768 devices in a mesh: dp: 192 (over y, z_hi, x, core), expert: 4 (over z_lo).
Axes of the slice: x: 4, y: 8, z: 12 (z_hi: 3, z_lo: 4; z = z_hi * 4 + z_lo), core: 2. Of those that a mesh axis runs over, the one named last changes fastest.
Arguments:
- tokens: bfloat16 [49152, 6144], P(('dp', 'expert')), may hold values from -6 to 6
- expert_ids: int32 [49152, 2], P(('dp', 'expert')), may hold values from 0 to 7, all different within a row; in each aligned block of 64 rows (0 to 63, 64 to 127, ...) at most 18 rows name the same one
- gate_probs: float32 [49152, 2], P(('dp', 'expert')), may hold values from 0.2 to 1
- w_gate: bfloat16 [8, 64, 6144], P('expert'), may hold values from -0.078125 to 0.078125
- w_up: bfloat16 [8, 64, 6144], P('expert'), may hold values from -0.078125 to 0.078125
- w_down: bfloat16 [8, 64, 6144], P('expert'), may hold values from -0.75 to 0.75
- v_gate: bfloat16 [8, 64, 6144], P('expert'), may hold values from -0.078125 to 0.078125
- v_up: bfloat16 [8, 64, 6144], P('expert'), may hold values from -0.078125 to 0.078125
Outputs:
- curvature: float32 [6144, 1024], P('dp', 'expert')
The draws below stay inside these ranges and needn't reach their ends.
Inputs may be any that keep to these rules, and one draw needn't show every extreme that they name: `expert_ids`: each token names two different experts; among the 64 tokens of one device (aligned blocks in order) at most 18 name any one expert, a bound that some block reaches.
All inputs are finite; a program needn't handle non-finite values.
Results may differ from the reference program's by a relative error of at most 0.02.
Values may be sent and summed in bfloat16 or wider, within the bound.
A program may use at most 64 MiB of HBM per device.

```python
import math
import jax
import jax.numpy as jnp
import numpy as np
from jax import lax

D = 6144
BLK = 64
TOK_DEV = 64
EXPERTS = 8
CAP = 18
TOKENS = 49152


def block_scale(rng, dims, pieces, least, top_value):
    def one(position, shards_of):
        draws = jax.random.uniform(jax.random.fold_in(jax.random.fold_in(rng, 6), position), (shards_of,), jnp.float32, least / len(pieces), top_value / len(pieces))
        return jnp.repeat(jnp.exp(draws), dims[position] // shards_of).reshape((-1,) + (1,) * (len(dims) - position - 1))

    level = one(*pieces[0])
    for cut in pieces[1:]:
        level = level * one(*cut)
    return level


def shared_out(key, own, number, rows, number_of, top, bound, skew):
    ranking = jax.random.permutation(key, number_of)
    crowded, common = shares(number_of, rows * top, bound, skew, True), shares(number_of, rows * top, bound, skew, False)
    places = jnp.arange(number_of)

    def named(tallies, rotation):
        used = int((tallies > 0).sum())
        fixed = max(1, used // 4)
        passed = fixed + (places - fixed + rotation * (used - fixed)) % max(1, number_of - fixed)
        return jnp.zeros((number_of,), jnp.int32).at[ranking[jnp.where(places < fixed, places, passed)]].set(jnp.asarray(tallies, jnp.int32))

    tallies = jnp.where(number % 4 == 0, named(crowded, number // 4), named(common, number - number // 4 - 1))
    mixed = jax.random.permutation(jax.random.fold_in(own, 3), number_of)
    donor, receiver = mixed[0:number_of // 2 * 2:2], mixed[1:number_of // 2 * 2:2]
    margin = jnp.minimum(tallies[donor] - 1, bound - tallies[receiver]) // 2
    margin = jnp.where((donor == ranking[0]) | (receiver == ranking[0]) | (tallies[receiver] == 0), 0, jnp.maximum(margin, 0))
    passed = jax.random.randint(jax.random.fold_in(own, 4), (number_of // 2,), 0, 1 << 20) % (margin + 1)
    tallies = tallies.at[donor].add(-passed).at[receiver].add(passed)
    items = jnp.searchsorted(jnp.cumsum(tallies), jnp.arange(rows * top), side="right").astype(jnp.int32)
    listing = items.reshape(top, rows).T
    listing = listing[jax.random.permutation(jax.random.fold_in(own, 1), rows)]
    rotation = jax.random.randint(jax.random.fold_in(own, 2), (rows, 1), 0, top)
    return jnp.take_along_axis(listing, (jnp.arange(top)[None, :] + rotation) % top, axis=1)


def shares(count, total, limit, skew, full):
    weights = [(1 << 20) // math.isqrt(standing ** skew) + 1 for standing in range(1, count + 1)]
    largest = limit if full else min(limit, max(-(-total // count), total * weights[0] // sum(weights)))
    least = 1 if total - largest >= count - 1 else 0
    counts, surplus = [largest] + [least] * (count - 1), total - largest - least * (count - 1)
    while surplus > 0:
        movable = [i for i in range(1, count) if counts[i] < largest] or [i for i in range(1, count) if counts[i] < limit]
        pool, left = sum([weights[i] for i in movable]), surplus
        for i in movable:
            more = min(limit - counts[i], max(1, left * weights[i] // pool), surplus)
            counts[i] = counts[i] + more
            surplus = surplus - more
    return np.array(counts)


def centred(key, shape, deviation, most, shards=(), held_as=jnp.bfloat16):
    values = jax.random.normal(key, shape, jnp.float32) * deviation
    if len(shards) > 0:
        values = block_scale(key, shape, shards, -0.22, 0.18) * values
    return jnp.clip(values, min=-most, max=most).astype(held_as)


def setup_inputs(seed: int = 0) -> dict:
    key_of = jax.random.split(jax.random.key(seed), 9)
    tokens = centred(key_of[0], (TOKENS, D), 1.0, 6.0, ((0, 768),))
    expert_ids_keys = jax.random.split(jax.random.fold_in(key_of[1], 1), TOKENS // TOK_DEV)
    expert_ids_turns = jax.random.permutation(jax.random.fold_in(key_of[1], 3), TOKENS // TOK_DEV)
    expert_ids = jax.vmap(lambda own, number: shared_out(jax.random.fold_in(key_of[1], 2), own, number, TOK_DEV, EXPERTS, 2, CAP, 1))(expert_ids_keys, expert_ids_turns).reshape((TOKENS, 2))
    gate_probs = jnp.clip(0.2 + 0.8 * jax.random.uniform(key_of[2], (TOKENS, 2), jnp.float32) ** block_scale(key_of[2], (TOKENS, 2), ((0, 768),), -0.2, 0.2), 0.2, 1.0)
    w_gate = centred(key_of[3], (EXPERTS, BLK, D), D ** -0.5, 0.078125, ((0, 4),))
    w_up = centred(key_of[4], (EXPERTS, BLK, D), D ** -0.5, 0.078125, ((0, 4),))
    w_down = centred(key_of[5], (EXPERTS, BLK, D), BLK ** -0.5, 0.75, ((0, 4),))
    v_gate = centred(key_of[6], (EXPERTS, BLK, D), D ** -0.5, 0.078125, ((0, 4),))
    v_up = centred(key_of[7], (EXPERTS, BLK, D), D ** -0.5, 0.078125, ((0, 4),))
    return {"tokens": tokens, "expert_ids": expert_ids, "gate_probs": gate_probs, "w_gate": w_gate, "w_up": w_up, "w_down": w_down, "v_gate": v_gate, "v_up": v_up}


def local_terms(pre_act, width):
    gate_pre = pre_act[:, :width]
    up_pre = pre_act[:, width:2 * width]
    gate_tan = pre_act[:, 2 * width:3 * width]
    up_tan = pre_act[:, 3 * width:]
    sigmoid = jax.nn.sigmoid(gate_pre)
    silu_val = gate_pre * sigmoid
    slope = sigmoid * (1.0 + gate_pre * (1.0 - sigmoid))
    hidden_tan = slope * up_pre * gate_tan + silu_val * up_tan
    return silu_val, slope * up_pre, hidden_tan


def reference(tokens, expert_ids, gate_probs, w_gate, w_up, w_down, v_gate, v_up):
    assigned = 2 * TOKENS
    blocks = TOKENS // TOK_DEV
    flat_ids = expert_ids.reshape(assigned).astype(jnp.int32)
    flat_probs = gate_probs.reshape(assigned)
    grouped = flat_ids.reshape(blocks, 2 * TOK_DEV)
    expert_hot = (grouped[:, :, None] == jnp.arange(EXPERTS, dtype=jnp.int32)[None, None, :]).astype(jnp.int32)
    before = (jnp.cumsum(expert_hot, axis=1) - expert_hot).astype(jnp.int32)
    slot_pos = jnp.sum(before * expert_hot, axis=2).astype(jnp.int32).reshape(assigned)
    owner = (jnp.arange(assigned, dtype=jnp.int32) // (2 * TOK_DEV)).astype(jnp.int32)
    table = jnp.full((EXPERTS, blocks, CAP), assigned, dtype=jnp.int32)
    table = table.at[flat_ids, owner, slot_pos].set(jnp.arange(assigned, dtype=jnp.int32))
    table = table.reshape(EXPERTS, blocks * CAP)
    padded_tokens = jnp.concatenate([tokens, jnp.zeros((1, D), tokens.dtype)], axis=0)
    padded_probs = jnp.concatenate([flat_probs, jnp.zeros((1,), flat_probs.dtype)], axis=0)
    stacked = jnp.concatenate([w_gate, w_up, v_gate, v_up], axis=1)

    def forward(index):
        picked = table[index]
        rows_here = padded_tokens[picked // 2]
        probs_here = padded_probs[picked]
        pre_act = jnp.dot(rows_here, stacked[index].T, preferred_element_type=jnp.float32)
        silu_val, slope_up, hidden_tan = local_terms(pre_act, BLK)
        scaled = (probs_here[:, None] * hidden_tan).astype(jnp.bfloat16)
        term_rows = jnp.dot(scaled, w_down[index], preferred_element_type=jnp.float32).astype(jnp.bfloat16)
        return term_rows, pre_act

    slot_terms, pre_all = lax.map(forward, jnp.arange(EXPERTS, dtype=jnp.int32))
    where_slot = (flat_ids * (blocks * CAP) + owner * CAP + slot_pos).astype(jnp.int32)
    term_assign = slot_terms.reshape(EXPERTS * blocks * CAP, D)[where_slot]
    adjoint = jnp.sum(term_assign.astype(jnp.float32).reshape(TOKENS, 2, D), axis=1).astype(jnp.bfloat16)
    padded_adjoint = jnp.concatenate([adjoint, jnp.zeros((1, D), adjoint.dtype)], axis=0)

    def backward(index):
        picked = table[index]
        rows_here = padded_tokens[picked // 2]
        probs_here = padded_probs[picked]
        silu_val, slope_up, hidden_tan = local_terms(pre_all[index], BLK)
        adjoint_here = padded_adjoint[picked // 2]
        pulled = jnp.dot(adjoint_here, w_down[index].T, preferred_element_type=jnp.float32)
        weighted = probs_here[:, None] * pulled
        coef = jnp.concatenate([(weighted * slope_up).astype(jnp.bfloat16), (weighted * silu_val).astype(jnp.bfloat16)], axis=1)
        return jnp.dot(rows_here.T, coef, preferred_element_type=jnp.float32) / TOKENS

    result = lax.map(backward, jnp.arange(EXPERTS, dtype=jnp.int32))
    return jnp.transpose(result, (1, 0, 2)).reshape(D, EXPERTS * 2 * BLK)
```

```python
import functools

import jax
import jax.numpy as jnp
from jax import lax
from jax.experimental import pallas as pl
from jax.experimental.pallas import tpu as pltpu
from jax.sharding import PartitionSpec as P

F32 = jnp.float32
BF16 = jnp.bfloat16
GRID = (8, 3, 4, 2)


def iota(shape, dim):
    return lax.broadcasted_iota(jnp.int32, shape, dim)


def dot(a, b, dims=((1,), (0,)), precision=None):
    return lax.dot_general(a, b, (dims, ((), ())), precision=precision, preferred_element_type=F32)


def one_hot(mask):
    return jnp.where(mask, 1.0, 0.0).astype(BF16)


def kernel(
    cfg,
    meta_ref, tokens_ref, part_ref, wg_ref, wu_ref, vg_ref, vu_ref, wd_ref,
    out_ref,
    meta_all, parts, weights, down, sent, sent_tail, rows, tails, pre, g_all, g_own,
    scaled_all, partial, core_send, core_recv, z_acc, z_send, z_recv,
    ax_s, ax_r, ay_s, ay_r, bx_s, bx_r, by_s, by_r,
    w_sem, meta_sem, part_sem, row_sem, tail_sem, sc_sem, core_sem, g_sem, rs_sem, z_sem,
):
    ny, nz, nx, nc, ne, cap = cfg
    width = tokens_ref.shape[1]
    slots = 2 * cap
    main = slots // 16 * 16
    rest = slots - main
    chunks = 16 // rest
    cw = width // chunks
    n_rows = ne * slots
    n_main = ne * main
    plane = ny * nx * nc
    r2 = 128 // plane
    g_parts = 16 // r2
    pw = width // g_parts

    dp = lax.axis_index("dp")
    e = lax.axis_index("expert")
    c = lax.rem(dp, nc)
    x = lax.rem(dp // nc, nx)
    zh = lax.rem(dp // (nc * nx), nz)
    y = dp // (nc * nx * nz)

    def at(yy=y, zz=zh, xx=x, cc=c):
        return ((yy * nz + zz) * nx + xx) * nc + cc

    def turn(v, k, n):
        return lax.rem(v + k + n, n)

    def remote(src, dst, s_sem, r_sem, dev):
        copy = pltpu.make_async_remote_copy(
            src_ref=src, dst_ref=dst, send_sem=s_sem, recv_sem=r_sem,
            device_id=dev, device_id_type=pl.DeviceIdType.MESH,
        )
        copy.start()
        return copy

    pending = []

    w_copies = []
    for m, ref in enumerate((wg_ref, wu_ref, vg_ref, vu_ref)):
        cp = pltpu.make_async_copy(ref, weights.at[pl.ds(m * 128, 128)], w_sem.at[m])
        cp.start()
        w_copies.append(cp)
    down_copy = pltpu.make_async_copy(wd_ref, down, w_sem.at[4])
    down_copy.start()

    peers = [(dp, turn(e, k, ne)) for k in range(1, ne)]
    for k in sorted({1, ny - 1} - {0}):
        peers.append((at(yy=turn(y, k, ny)), e))
    for k in sorted({1, nx - 1} - {0}):
        peers.append((at(xx=turn(x, k, nx)), e))
    for k in range(1, nz):
        peers.append((at(zz=turn(zh, k, nz)), e))
    for k in range(1, nc):
        peers.append((at(cc=turn(c, k, nc)), e))
    barrier = pltpu.get_barrier_semaphore()
    for dev in peers:
        pl.semaphore_signal(barrier, inc=1, device_id=dev, device_id_type=pl.DeviceIdType.MESH)
    pl.semaphore_wait(barrier, len(peers))

    meta_copies, part_copies = [], []
    for k in range(1, ne):
        dev = (dp, turn(e, k, ne))
        meta_copies.append(remote(meta_ref, meta_all.at[e], meta_sem.at[0, k - 1], meta_sem.at[1, k - 1], dev))
    for k in range(1, ne):
        dev = (dp, turn(e, k, ne))
        part_copies.append(remote(part_ref, parts.at[e], part_sem.at[0, k - 1], part_sem.at[1, k - 1], dev))
    meta_all[e] = meta_ref[...]
    parts[e] = part_ref[...]

    lanes = 128
    upper = one_hot(iota((lanes, lanes), 0) < iota((lanes, lanes), 1))

    def slot_of(meta):
        ids = meta[0:1, :].astype(jnp.int32)
        hot = iota((2 * ne, lanes), 0) == ids
        before = dot(one_hot(hot), upper)
        where = before + cap * iota((2 * ne, lanes), 0).astype(F32)
        return jnp.sum(jnp.where(hot, where, 0.0), axis=0, keepdims=True).astype(jnp.int32)

    g_mine = slot_of(meta_ref[...])
    half = one_hot((iota((lanes, lanes // 2), 0) >> 1) == iota((lanes, lanes // 2), 1))
    r_main = iota((n_main, lanes), 0)
    slot_main = (r_main // main) * slots + r_main % main
    pick_main = dot(one_hot(slot_main == g_mine), half).astype(BF16)
    n_tail = ne * 16
    r_tail = iota((n_tail, lanes), 0)
    slot_tail = (r_tail // 16) * slots + main + r_tail % rest
    q_tail = (r_tail % 16) // rest
    hit_tail = slot_tail == g_mine
    tail_val = jnp.zeros((n_tail, cw), F32)
    for q in range(chunks):
        pick = dot(one_hot(hit_tail & (q_tail == q)), half).astype(BF16)
        tail_val = tail_val + dot(pick, tokens_ref[:, q * cw : (q + 1) * cw])
    tail_val = tail_val.astype(BF16)
    for d in range(ne):
        sent_tail[d] = tail_val[d * 16 : (d + 1) * 16]
    tail_copies = []
    row_copies = []
    for q in range(chunks):
        cols = slice(q * cw, (q + 1) * cw)
        val = dot(pick_main, tokens_ref[:, cols]).astype(BF16)
        for d in range(ne):
            sent[d, :, cols] = val[d * main : (d + 1) * main]
        got = []
        for k in (2, 1, 3) if ne == 4 else range(1, ne):
            d = turn(e, k, ne)
            got.append(
                remote(
                    sent.at[d, :, pl.ds(q * cw, cw)],
                    rows.at[pl.ds(pl.multiple_of(e * main, 16), main), pl.ds(q * cw, cw)],
                    row_sem.at[0, q, k - 1], row_sem.at[1, q, k - 1], (dp, d),
                )
            )
            if q == 0:
                tail_copies.append(
                    remote(sent_tail.at[d], tails.at[e], tail_sem.at[0, k - 1], tail_sem.at[1, k - 1], (dp, d))
                )
        row_copies.append(got)
        rows[pl.ds(pl.multiple_of(e * main, 16), main), cols] = sent[e, :, cols]
    tails[e] = sent_tail[e]

    down_copy.wait()
    for cp in part_copies:
        cp.wait()
    gw = parts[...].reshape(ne * 16, pw)
    acc = jnp.zeros((ne * 16, 128), F32)
    r_part = iota((ne * 16, 128), 0) % 16 // r2
    for i in range(g_parts):
        acc = acc + jnp.where(r_part == i, dot(gw, down[:, i * pw : (i + 1) * pw], ((1,), (1,))), 0.0)
    g_rows = ne * r2
    to_row = iota((g_rows, ne * 16), 0)
    from_row = iota((g_rows, ne * 16), 1)
    collect = jnp.where((from_row // 16 == to_row // r2) & (from_row % r2 == to_row % r2), 1.0, 0.0)
    g_all[y, x, c] = dot(collect, acc, precision=lax.Precision.HIGHEST)

    def gather(block, me, n, dev, base):
        right = n // 2
        left = n - 1 - right
        r_cp, l_cp = [], []
        if right:
            r_cp.append(remote(block(me), block(me), g_sem.at[0, base], g_sem.at[1, base], dev(1)))
        if left:
            l_cp.append(remote(block(me), block(me), g_sem.at[0, base + 4], g_sem.at[1, base + 4], dev(-1)))
        for k in range(right):
            r_cp[k].wait_recv()
            if k + 1 < right:
                b = block(turn(me, -1 - k, n))
                s = base + k + 1
                r_cp.append(remote(b, b, g_sem.at[0, s], g_sem.at[1, s], dev(1)))
            if k < left:
                l_cp[k].wait_recv()
                if k + 1 < left:
                    b = block(turn(me, 1 + k, n))
                    s = base + 4 + k + 1
                    l_cp.append(remote(b, b, g_sem.at[0, s], g_sem.at[1, s], dev(-1)))
        pending.extend(r_cp + l_cp)

    gather(lambda i: g_all.at[y, x, i], c, nc, lambda k: (at(cc=turn(c, k, nc)), e), 0)
    gather(lambda i: g_all.at[y, i], x, nx, lambda k: (at(xx=turn(x, k, nx)), e), 8)
    gather(lambda i: g_all.at[i], y, ny, lambda k: (at(yy=turn(y, k, ny)), e), 16)

    for cp in meta_copies:
        cp.wait()
    r_all = iota((n_rows, lanes), 0)
    in_main = r_all < n_main
    src_all = jnp.where(in_main, r_all // main, (r_all - n_main) // rest)
    slot_all = jnp.where(in_main, r_all % main, main + (r_all - n_main) % rest)
    same = one_hot((iota((lanes, lanes), 0) >> 1) == (iota((lanes, lanes), 1) >> 1))
    g_src = [slot_of(meta_all[s]) for s in range(ne)]
    prob = jnp.zeros((n_rows, 1), F32)
    mine = []
    for s in range(ne):
        hit = (src_all == s) & (slot_all + e * slots == g_src[s])
        prob = prob + jnp.sum(jnp.where(hit, meta_all[s][1:2, :], 0.0), axis=1, keepdims=True)
        mine.append(dot(one_hot(hit), same).astype(BF16))
    links = []
    for q in range(ne):
        total = jnp.zeros((n_rows, n_rows), F32)
        for s in range(ne):
            hit = one_hot((src_all == s) & (slot_all + q * slots == g_src[s]))
            total = total + dot(mine[s], hit, ((1,), (1,)))
        links.append(total.astype(BF16))
    flat_g = g_all[...].reshape(plane * g_rows, 128).astype(BF16)
    p_row = iota((128, plane * g_rows), 0)
    p_col = iota((128, plane * g_rows), 1)
    for q in range(ne):
        perm = one_hot(p_col == (p_row // r2) * g_rows + q * r2 + p_row % r2)
        g_own[q] = dot(perm, flat_g).astype(BF16)

    for cp in w_copies:
        cp.wait()
    for cp in tail_copies:
        cp.wait()
    t_row = iota((ne * rest, n_tail), 0)
    t_col = iota((ne * rest, n_tail), 1)
    flat_tails = tails[...].reshape(n_tail, cw)
    for q in range(chunks):
        hit = (t_row // rest == t_col // 16) & (t_col % 16 == q * rest + t_row % rest)
        rows[n_main:n_rows, q * cw : (q + 1) * cw] = dot(one_hot(hit), flat_tails).astype(BF16)
    for q in range(chunks):
        for cp in row_copies[q]:
            cp.wait()
        cols = slice(q * cw, (q + 1) * cw)
        val = dot(rows[:, cols], weights[:, cols], ((1,), (1,)))
        if q == 0:
            pre[...] = val
        else:
            pre[...] += val

    gate_pre, up_pre = pre[:, 0:128], pre[:, 128:256]
    gate_tan, up_tan = pre[:, 256:384], pre[:, 384:512]
    sigmoid = jax.nn.sigmoid(gate_pre)
    silu_val = gate_pre * sigmoid
    slope_up = sigmoid * (1.0 + gate_pre * (1.0 - sigmoid)) * up_pre
    hidden_tan = slope_up * gate_tan + silu_val * up_tan
    valid = (iota((n_rows, 128), 1) // 64) == jnp.where(slot_all >= cap, 1, 0)
    scaled_all[e] = jnp.where(valid, prob * hidden_tan, 0.0).astype(BF16)
    sc_copies = [
        remote(scaled_all.at[e], scaled_all.at[e], sc_sem.at[0, k - 1], sc_sem.at[1, k - 1], (dp, turn(e, k, ne)))
        for k in range(1, ne)
    ]
    for cp in sc_copies:
        cp.wait()
    pulled = jnp.zeros((n_rows, 128), F32)
    for q in range(ne):
        pulled = pulled + dot(dot(links[q], scaled_all[q]).astype(BF16), g_own[q])
    weighted = jnp.where(valid, prob * pulled, 0.0)
    coef_gate = weighted * slope_up
    coef_up = weighted * silu_val
    low = iota((n_rows, 128), 1) < 64
    coef = jnp.concatenate(
        [
            jnp.where(low, coef_gate, pltpu.roll(coef_up, 64, 1)),
            jnp.where(low, pltpu.roll(coef_gate, 64, 1), coef_up),
        ],
        axis=1,
    ).astype(BF16)

    span = width // ny
    own = width // (ny * nz * nx * nc)
    core_copies = []
    for i in range(ny):
        part = dot(rows[:, i * span : (i + 1) * span], coef, ((0,), (0,)))
        partial[i] = part.reshape(nz, nx, nc, own, 256)
        if nc == 2:
            core_send[i] = partial[i, :, :, 1 - c].astype(BF16)
            core_copies.append(
                remote(core_send.at[i], core_recv.at[i], core_sem.at[0, i], core_sem.at[1, i], (at(cc=1 - c), e))
            )
    for cp in core_copies:
        cp.wait()
    for i in range(ny if nc == 2 else 0):
        partial[i, :, :, c] += core_recv[i].astype(F32)

    def ring(own_block, me, n, dev, s_buf, r_buf, base, long_right):
        right = n // 2 if long_right else n - 1 - n // 2
        left = n - 1 - right
        r_cp, l_cp = [], []
        for k in range(max(right, left)):
            if k < right:
                val = own_block(turn(me, right - k, n))
                if k:
                    r_cp[k - 1].wait_recv()
                    val = val + r_buf[k - 1].astype(F32)
                s_buf[k] = val.astype(BF16)
                r_cp.append(remote(s_buf.at[k], r_buf.at[k], rs_sem.at[0, base + k], rs_sem.at[1, base + k], dev(1)))
            if k < left:
                j = right + k
                val = own_block(turn(me, k - left, n))
                if k:
                    l_cp[k - 1].wait_recv()
                    val = val + r_buf[j - 1].astype(F32)
                s_buf[j] = val.astype(BF16)
                l_cp.append(remote(s_buf.at[j], r_buf.at[j], rs_sem.at[0, base + j], rs_sem.at[1, base + j], dev(-1)))
            yield None
        total = own_block(me)
        if right:
            r_cp[-1].wait_recv()
            total = total + r_buf[right - 1].astype(F32)
        if left:
            l_cp[-1].wait_recv()
            total = total + r_buf[right + left - 1].astype(F32)
        pending.extend(r_cp + l_cp)
        yield total

    dev_x = lambda k: (at(xx=turn(x, k, nx)), e)
    dev_y = lambda k: (at(yy=turn(y, k, ny)), e)

    def path_a():
        for total in ring(lambda t: partial[:, :, t, c, :, 0:128], x, nx, dev_x, ax_s, ax_r, 0, True):
            if total is None:
                yield
        partial[:, :, x, c, :, 0:128] = total
        for total in ring(lambda t: partial[t, :, x, c, :, 0:128], y, ny, dev_y, ay_s, ay_r, 4, False):
            if total is None:
                yield
        z_acc[:, :, 0:128] = total

    def path_b():
        for total in ring(lambda t: partial[t, :, :, c, :, 128:256], y, ny, dev_y, by_s, by_r, 12, True):
            if total is None:
                yield
        partial[y, :, :, c, :, 128:256] = total
        for total in ring(lambda t: partial[y, :, t, c, :, 128:256], x, nx, dev_x, bx_s, bx_r, 20, False):
            if total is None:
                yield
        z_acc[:, :, 128:256] = total

    live = [path_b(), path_a()]
    while live:
        for path in list(live):
            try:
                next(path)
            except StopIteration:
                live.remove(path)

    result = z_acc[zh]
    z_copies = []
    for k in range(1, nz):
        t = turn(zh, k, nz)
        z_send[k - 1] = z_acc[t].astype(BF16)
        z_copies.append(
            remote(z_send.at[k - 1], z_recv.at[k - 1], z_sem.at[0, k - 1], z_sem.at[1, k - 1], (at(zz=t), e))
        )
    for k, cp in enumerate(z_copies):
        cp.wait()
        result = result + z_recv[k].astype(F32)
    out_ref[...] = result
    for cp in pending:
        cp.wait_send()


def fused(cfg, meta, tokens, part, mats):
    ny, nz, nx, nc, ne, cap = cfg
    width = tokens.shape[1]
    slots = 2 * cap
    main = slots // 16 * 16
    rest = slots - main
    chunks = 16 // rest
    n_rows = ne * slots
    plane = ny * nx * nc
    r2 = 128 // plane
    own = width // (ny * nz * nx * nc)
    vmem, dma = pltpu.VMEM, pltpu.SemaphoreType.DMA
    vspec = pl.BlockSpec(memory_space=pltpu.VMEM)
    hspec = pl.BlockSpec(memory_space=pl.ANY)
    hx, hy = max(nx - 1, 1), max(ny - 1, 1)
    return pl.pallas_call(
        functools.partial(kernel, cfg),
        out_shape=jax.ShapeDtypeStruct((own, 256), F32),
        in_specs=[vspec] * 3 + [hspec] * 5,
        out_specs=vspec,
        scratch_shapes=[
            vmem((ne, 8, 128), F32),
            vmem((ne,) + part.shape, BF16),
            vmem((512, width), BF16),
            vmem((128, width), BF16),
            vmem((ne, main, width), BF16),
            vmem((ne, 16, width // chunks), BF16),
            vmem((n_rows, width), BF16),
            vmem((ne, 16, width // chunks), BF16),
            vmem((n_rows, 512), F32),
            vmem((ny, nx, nc, ne * r2, 128), F32),
            vmem((ne, 128, 128), BF16),
            vmem((ne, n_rows, 128), BF16),
            vmem((ny, nz, nx, nc, own, 256), F32),
            vmem((ny, nz, nx, own, 256), BF16),
            vmem((ny, nz, nx, own, 256), BF16),
            vmem((nz, own, 256), F32),
            vmem((max(nz - 1, 1), own, 256), BF16),
            vmem((max(nz - 1, 1), own, 256), BF16),
            vmem((hx, ny, nz, own, 128), BF16),
            vmem((hx, ny, nz, own, 128), BF16),
            vmem((hy, nz, own, 128), BF16),
            vmem((hy, nz, own, 128), BF16),
            vmem((hx, nz, own, 128), BF16),
            vmem((hx, nz, own, 128), BF16),
            vmem((hy, nz, nx, own, 128), BF16),
            vmem((hy, nz, nx, own, 128), BF16),
            dma((5,)),
            dma((2, ne - 1)),
            dma((2, ne - 1)),
            dma((2, chunks, ne - 1)),
            dma((2, ne - 1)),
            dma((2, ne - 1)),
            dma((2, ny)),
            dma((2, 24)),
            dma((2, 24)),
            dma((2, max(nz - 1, 1))),
        ],
        compiler_params=pltpu.CompilerParams(
            collective_id=0, has_side_effects=True, vmem_limit_bytes=58 * 2**20
        ),
    )(meta, tokens, part, *mats)


def body(cfg, tokens, expert_ids, gate_probs, w_gate, w_up, w_down, v_gate, v_up):
    ny, nz, nx, nc, ne, cap = cfg
    width = tokens.shape[1]
    total_tokens = tokens.shape[0] * ny * nz * nx * nc * ne
    meta = jnp.stack([expert_ids.reshape(-1).astype(F32), gate_probs.reshape(-1)])
    meta = jnp.pad(meta, ((0, 6), (0, 0)))
    mats = [w.reshape(128, width) for w in (w_gate, w_up, v_gate, v_up, w_down)]
    dp = lax.axis_index("dp")
    place = (dp // (nc * nx * nz)) * (nx * nc) + dp % (nx * nc)
    r2 = 128 // (ny * nx * nc)
    part = lax.dynamic_slice(mats[4], (place * r2, 0), (r2, width))
    part = part.reshape(r2, 16 // r2, width * r2 // 16).transpose(1, 0, 2).reshape(16, -1)
    return fused(cfg, meta, tokens, part, mats) * (1.0 / total_tokens)


def solution(mesh, grid=GRID):
    cfg = grid + (mesh.shape["expert"], 18)
    return jax.shard_map(
        functools.partial(body, cfg),
        mesh=mesh,
        in_specs=(
            P(("dp", "expert"), None),
            P(("dp", "expert"), None),
            P(("dp", "expert"), None),
            P("expert", None, None),
            P("expert", None, None),
            P("expert", None, None),
            P("expert", None, None),
            P("expert", None, None),
        ),
        out_specs=P("dp", "expert"),
        check_vma=False,
    )
```

```python
import functools

import jax
import jax.numpy as jnp
from jax import lax
from jax.experimental import pallas as pl
from jax.experimental.pallas import tpu as pltpu
from jax.sharding import PartitionSpec as P

F32 = jnp.float32
BF16 = jnp.bfloat16
GRID = (8, 3, 4, 2)


def iota(shape, dim):
    return lax.broadcasted_iota(jnp.int32, shape, dim)


def dot(a, b, dims=((1,), (0,)), precision=None):
    return lax.dot_general(a, b, (dims, ((), ())), precision=precision, preferred_element_type=F32)


def one_hot(mask):
    return jnp.where(mask, 1.0, 0.0).astype(BF16)


def kernel(
    cfg,
    ids_ref, probs_ref, tokens_ref, wg_ref, wu_ref, vg_ref, vu_ref, wd_ref,
    out_ref,
    meta_own, meta_all, part_own, parts, raw, weights, down, ordered, sent, sent_tail, rows, tails, pre,
    g_all, g_own, scaled_all, gathered, coef_all, coefs, partial, core_send, core_recv,
    z_acc, z_send, z_recv, ring_s, ring_r,
    w_sem, meta_sem, part_sem, row_sem, tail_sem, x_sem, sc_sem, coef_sem, core_sem, g_sem, rs_sem, z_sem,
):
    ny, nz, nx, nc, ne, cap = cfg
    width = tokens_ref.shape[1]
    slots = 2 * cap
    main = slots // 16 * 16
    rest = slots - main
    tail_parts = 16 // rest
    tw = width // tail_parts
    cw = width // nx
    n_rows = ne * slots
    n_main = ne * main
    n_tail = ne * 16
    plane = ny * nx * nc
    r2 = 128 // plane
    g_parts = 16 // r2
    pw = width // g_parts
    own = width // (ny * nz * nx * nc)

    dp = lax.axis_index("dp")
    e = lax.axis_index("expert")
    c = lax.rem(dp, nc)
    x = lax.rem(dp // nc, nx)
    zh = lax.rem(dp // (nc * nx), nz)
    y = dp // (nc * nx * nz)

    def at(yy=y, zz=zh, xx=x, cc=c):
        return ((yy * nz + zz) * nx + xx) * nc + cc

    def turn(v, k, n):
        return lax.rem(v + k + n, n)

    def remote(src, dst, s_sem, r_sem, dev):
        copy = pltpu.make_async_remote_copy(
            src_ref=src, dst_ref=dst, send_sem=s_sem, recv_sem=r_sem,
            device_id=dev, device_id_type=pl.DeviceIdType.MESH,
        )
        copy.start()
        return copy

    w_copies = []
    for m, ref in enumerate((wg_ref, wu_ref, vg_ref, vu_ref)):
        cp = pltpu.make_async_copy(ref, raw.at[pl.ds(m * 128, 128)], w_sem.at[m])
        cp.start()
        w_copies.append(cp)
    down_copy = pltpu.make_async_copy(wd_ref, down, w_sem.at[4])
    down_copy.start()

    peers = [(dp, turn(e, k, ne)) for k in range(1, ne)]
    for k in range(1, ny):
        peers.append((at(yy=turn(y, k, ny)), e))
    for k in range(1, nx):
        peers.append((at(xx=turn(x, k, nx)), e))
    for k in range(1, nz):
        peers.append((at(zz=turn(zh, k, nz)), e))
    for k in range(1, nc):
        peers.append((at(cc=turn(c, k, nc)), e))
    barrier = pltpu.get_barrier_semaphore()
    for dev in peers:
        pl.semaphore_signal(barrier, inc=1, device_id=dev, device_id_type=pl.DeviceIdType.MESH)

    lanes = 128
    upper = one_hot(iota((lanes, lanes), 0) < iota((lanes, lanes), 1))

    def slot_of(meta):
        ids = meta[0:1, :].astype(jnp.int32)
        hot = iota((2 * ne, lanes), 0) == ids
        before = dot(one_hot(hot), upper)
        where = before + cap * iota((2 * ne, lanes), 0).astype(F32)
        return jnp.sum(jnp.where(hot, where, 0.0), axis=0, keepdims=True).astype(jnp.int32)

    ids = ids_ref[...].astype(F32)
    probs = probs_ref[...]
    meta = jnp.concatenate(
        [
            jnp.concatenate([ids[0:1, :], ids[1:2, :]], axis=1),
            jnp.concatenate([probs[0:1, :], probs[1:2, :]], axis=1),
            jnp.zeros((6, lanes), F32),
        ],
        axis=0,
    )
    meta_own[...] = meta
    meta_all[e] = meta
    g_mine = slot_of(meta)
    half = one_hot(iota((lanes, lanes // 2), 0) % 64 == iota((lanes, lanes // 2), 1))
    r_main = iota((n_main, lanes), 0)
    slot_main = (r_main // main) * slots + r_main % main
    pick_main = dot(one_hot(slot_main == g_mine), half).astype(BF16)
    r_tail = iota((n_tail, lanes), 0)
    slot_tail = (r_tail // 16) * slots + main + r_tail % rest
    q_tail = (r_tail % 16) // rest
    hit_tail = slot_tail == g_mine

    def reorder(src, dst, rows_of):
        low = iota((rows_of, 128), 1) < 64

        def pair(m, carry):
            for h in range(nx // 2):
                first = src[:, pl.ds(pl.multiple_of((2 * m * (nx // 2) + h) * 128, 128), 128)]
                second = src[:, pl.ds(pl.multiple_of(((2 * m + 1) * (nx // 2) + h) * 128, 128), 128)]
                dst[:, pl.ds(pl.multiple_of(2 * h * cw + m * 128, 128), 128)] = jnp.where(
                    low, first, pltpu.roll(second, 64, 1)
                )
                dst[:, pl.ds(pl.multiple_of((2 * h + 1) * cw + m * 128, 128), 128)] = jnp.where(
                    low, pltpu.roll(first, 64, 1), second
                )
            return carry

        lax.fori_loop(0, ny * nz // 2, pair, 0)

    reorder(tokens_ref, ordered, tokens_ref.shape[0])

    order = [2, 1, 3, 0] if nx == 4 else list(range(1, nx)) + [0]
    z_order = (2, 1, 3) if ne == 4 else tuple(range(1, ne))

    def columns(k):
        return pl.ds(pl.multiple_of(turn(x, k, nx) * cw, 128), cw)

    def place_rows(k):
        val = dot(pick_main, ordered[:, columns(k)]).astype(BF16)
        for d in range(ne):
            sent[d, :, columns(k)] = val[d * main : (d + 1) * main]

    my_rows = pl.ds(pl.multiple_of(e * main, 16), main)

    def send_rows(k):
        got = []
        for j in z_order:
            d = turn(e, j, ne)
            got.append(
                remote(
                    sent.at[d, :, columns(k)], rows.at[my_rows, columns(k)],
                    row_sem.at[0, k, j - 1], row_sem.at[1, k, j - 1], (dp, d),
                )
            )
        rows[my_rows, columns(k)] = sent[e, :, columns(k)]
        return got

    place_rows(order[0])
    pl.semaphore_wait(barrier, len(peers))

    meta_copies, tail_copies, part_copies, row_copies = [], [], [], {}
    for j in range(1, ne):
        meta_copies.append(
            remote(meta_own, meta_all.at[e], meta_sem.at[0, j - 1], meta_sem.at[1, j - 1], (dp, turn(e, j, ne)))
        )
    row_copies[order[0]] = send_rows(order[0])
    tail_val = jnp.zeros((n_tail, tw), F32)
    for q in range(tail_parts):
        pick = dot(one_hot(hit_tail & (q_tail == q)), half).astype(BF16)
        tail_val = tail_val + dot(pick, ordered[:, q * tw : (q + 1) * tw])
    tail_val = tail_val.astype(BF16)
    for d in range(ne):
        sent_tail[d] = tail_val[d * 16 : (d + 1) * 16]
    for j in z_order:
        d = turn(e, j, ne)
        tail_copies.append(
            remote(sent_tail.at[d], tails.at[e], tail_sem.at[0, j - 1], tail_sem.at[1, j - 1], (dp, d))
        )
    tails[e] = sent_tail[e]
    down_copy.wait()
    s_row = iota((16, 128), 0)
    s_col = iota((16, 128), 1)
    first = ((y * nx + x) * nc + c) * r2
    for i in range(g_parts):
        pick = one_hot((s_row // r2 == i) & (s_col == first + s_row % r2))
        val = dot(pick, down[:, i * pw : (i + 1) * pw])
        part_val = val if i == 0 else part_val + val
    part_own[...] = part_val.astype(BF16)
    parts[e] = part_own[...]
    for j in z_order:
        part_copies.append(
            remote(part_own, parts.at[e], part_sem.at[0, j - 1], part_sem.at[1, j - 1], (dp, turn(e, j, ne)))
        )
    for k in order[1:]:
        place_rows(k)
        row_copies[k] = send_rows(k)

    for cp in tail_copies:
        cp.wait()
    t_row = iota((ne * rest, n_tail), 0)
    t_col = iota((ne * rest, n_tail), 1)
    flat_tails = tails[...].reshape(n_tail, tw)
    for q in range(tail_parts):
        hit = (t_row // rest == t_col // 16) & (t_col % 16 == q * rest + t_row % rest)
        rows[n_main:n_rows, q * tw : (q + 1) * tw] = dot(one_hot(hit), flat_tails).astype(BF16)

    for cp in part_copies:
        cp.wait()
    gw = parts[...].reshape(ne * 16, pw)
    acc = jnp.zeros((ne * 16, 128), F32)
    r_part = iota((ne * 16, 128), 0) % 16 // r2
    for i in range(g_parts):
        acc = acc + jnp.where(r_part == i, dot(gw, down[:, i * pw : (i + 1) * pw], ((1,), (1,))), 0.0)
    g_rows = ne * r2
    to_row = iota((g_rows, ne * 16), 0)
    from_row = iota((g_rows, ne * 16), 1)
    collect = jnp.where((from_row // 16 == to_row // r2) & (from_row % r2 == to_row % r2), 1.0, 0.0)
    g_all[y, x, c] = dot(collect, acc, precision=lax.Precision.HIGHEST)

    def share(block, n, dev, base):
        return [
            remote(block, block, g_sem.at[0, base + k], g_sem.at[1, base + k], dev(k)) for k in range(1, n)
        ]

    def finish(copies):
        for cp in copies:
            cp.wait()

    x_rows = pl.ds(pl.multiple_of(x * n_rows, 16), n_rows)
    x_copies = []

    def forward(n):
        k = order[n]
        finish(row_copies[k])
        if k:
            x_copies.append(
                remote(
                    rows.at[:, columns(k)], gathered.at[x_rows], x_sem.at[0, k - 1], x_sem.at[1, k - 1],
                    (at(xx=turn(x, k, nx)), e),
                )
            )
        val = dot(rows[:, columns(k)], weights[:, columns(k)], ((1,), (1,)))
        if n == 0:
            pre[...] = val
        else:
            pre[...] += val

    g_copies = share(g_all.at[y, x, c], nc, lambda k: (at(cc=turn(c, k, nc)), e), 0)
    finish(w_copies)
    reorder(raw, weights, 512)
    forward(0)
    finish(g_copies)
    g_copies = share(g_all.at[y, x], nx, lambda k: (at(xx=turn(x, k, nx)), e), 8)
    for n in range(1, nx - 2):
        forward(n)
    finish(g_copies)
    g_copies = share(g_all.at[y], ny, lambda k: (at(yy=turn(y, k, ny)), e), 16)

    finish(meta_copies)
    r_all = iota((n_rows, lanes), 0)
    in_main = r_all < n_main
    src_all = jnp.where(in_main, r_all // main, (r_all - n_main) // rest)
    slot_all = jnp.where(in_main, r_all % main, main + (r_all - n_main) % rest)
    same = one_hot(iota((lanes, lanes), 0) % 64 == iota((lanes, lanes), 1) % 64)
    g_src = [slot_of(meta_all[s]) for s in range(ne)]
    prob = jnp.zeros((n_rows, 1), F32)
    mine = []
    for s in range(ne):
        hit = (src_all == s) & (slot_all + e * slots == g_src[s])
        prob = prob + jnp.sum(jnp.where(hit, meta_all[s][1:2, :], 0.0), axis=1, keepdims=True)
        mine.append(dot(one_hot(hit), same).astype(BF16))
    links = []
    for q in range(ne):
        total = jnp.zeros((n_rows, n_rows), F32)
        for s in range(ne):
            hit = one_hot((src_all == s) & (slot_all + q * slots == g_src[s]))
            total = total + dot(mine[s], hit, ((1,), (1,)))
        links.append(total.astype(BF16))

    if nx > 2:
        forward(nx - 2)
    finish(g_copies)
    flat_g = g_all[...].reshape(plane * g_rows, 128).astype(BF16)
    p_row = iota((128, plane * g_rows), 0)
    p_col = iota((128, plane * g_rows), 1)
    for q in range(ne):
        perm = one_hot(p_col == (p_row // r2) * g_rows + q * r2 + p_row % r2)
        g_own[q] = dot(perm, flat_g).astype(BF16)
    forward(nx - 1)

    gate_pre, up_pre = pre[:, 0:128], pre[:, 128:256]
    gate_tan, up_tan = pre[:, 256:384], pre[:, 384:512]
    sigmoid = jax.nn.sigmoid(gate_pre)
    silu_val = gate_pre * sigmoid
    slope_up = sigmoid * (1.0 + gate_pre * (1.0 - sigmoid)) * up_pre
    hidden_tan = slope_up * gate_tan + silu_val * up_tan
    valid = (iota((n_rows, 128), 1) // 64) == jnp.where(slot_all >= cap, 1, 0)
    scaled_all[e] = jnp.where(valid, prob * hidden_tan, 0.0).astype(BF16)
    sc_copies = [
        remote(scaled_all.at[e], scaled_all.at[e], sc_sem.at[0, k - 1], sc_sem.at[1, k - 1], (dp, turn(e, k, ne)))
        for k in range(1, ne)
    ]
    for cp in sc_copies:
        cp.wait()
    pulled = jnp.zeros((n_rows, 128), F32)
    for q in range(ne):
        pulled = pulled + dot(dot(links[q], scaled_all[q]).astype(BF16), g_own[q])
    weighted = jnp.where(valid, prob * pulled, 0.0)
    coef_gate = weighted * slope_up
    coef_up = weighted * silu_val
    low = iota((n_rows, 128), 1) < 64
    first_expert = slot_all < cap
    coef_all[x] = jnp.where(
        low,
        jnp.where(first_expert, coef_gate, pltpu.roll(coef_gate, 64, 1)),
        jnp.where(first_expert, pltpu.roll(coef_up, 64, 1), coef_up),
    ).astype(BF16)
    coef_copies = [
        remote(coef_all.at[x], coef_all.at[x], coef_sem.at[0, k - 1], coef_sem.at[1, k - 1], (at(xx=turn(x, k, nx)), e))
        for k in range(1, nx)
    ]
    gathered[x_rows] = rows[:, columns(0)]
    for cp in x_copies + coef_copies:
        cp.wait()
    for i in range(nx):
        val = coef_all[i]
        coefs[i * n_rows : (i + 1) * n_rows, 0:128] = jnp.where(first_expert, val, jnp.zeros_like(val))
        coefs[i * n_rows : (i + 1) * n_rows, 128:256] = jnp.where(first_expert, jnp.zeros_like(val), val)

    span = cw // ny
    half_y = y // 2
    parity = y % 2
    pairs = [2, 1, 3, 0] if ny == 8 else list(range(1, ny // 2)) + [0]
    core_copies, y_copies = {}, {}

    def product(m):
        i = lax.rem(half_y + m, ny // 2)
        lhs = gathered[:, pl.ds(pl.multiple_of(i * 2 * span, 128), 2 * span)]
        part = dot(lhs, coefs[...], ((0,), (0,)))
        both = pl.ds(2 * i, 2)
        partial[both] = part.reshape(2, nz, nc, own, 256)
        if nc == 2:
            core_send[both] = partial[both, :, 1 - c].astype(BF16)
            core_copies[m] = remote(
                core_send.at[both], core_recv.at[both], core_sem.at[0, m], core_sem.at[1, m], (at(cc=1 - c), e)
            )

    def summed(t):
        val = partial[t, :, c]
        return val + core_recv[t].astype(F32) if nc == 2 else val

    def send_on(m):
        i = lax.rem(half_y + m, ny // 2)
        if nc == 2:
            core_copies[m].wait()
        for b in (1, 0):
            t = 2 * i + (parity + b) % 2
            j = 2 * m + b
            if j == 0:
                z_acc[...] = summed(t)
            else:
                ring_s[j - 1] = summed(t).astype(BF16)
                y_copies[j] = remote(
                    ring_s.at[j - 1], ring_r.at[j - 1], rs_sem.at[0, j - 1], rs_sem.at[1, j - 1], (at(yy=t), e)
                )

    for n, m in enumerate(pairs):
        product(m)
        if n:
            send_on(pairs[n - 1])
    send_on(pairs[-1])
    total = z_acc[...]
    for j, cp in y_copies.items():
        cp.wait()
        total = total + ring_r[j - 1].astype(F32)
    z_acc[...] = total

    result = z_acc[zh]
    z_copies = []
    for k in range(1, nz):
        t = turn(zh, k, nz)
        z_send[k - 1] = z_acc[t].astype(BF16)
        z_copies.append(
            remote(z_send.at[k - 1], z_recv.at[k - 1], z_sem.at[0, k - 1], z_sem.at[1, k - 1], (at(zz=t), e))
        )
    for k, cp in enumerate(z_copies):
        cp.wait()
        result = result + z_recv[k].astype(F32)
    out_ref[...] = result


def fused(cfg, ids, probs, tokens, mats):
    ny, nz, nx, nc, ne, cap = cfg
    width = tokens.shape[1]
    slots = 2 * cap
    main = slots // 16 * 16
    tail_parts = 16 // (slots - main)
    n_rows = ne * slots
    r2 = 128 // (ny * nx * nc)
    own = width // (ny * nz * nx * nc)
    part = (16, width * r2 // 16)
    vmem, dma = pltpu.VMEM, pltpu.SemaphoreType.DMA
    vspec = pl.BlockSpec(memory_space=pltpu.VMEM)
    hspec = pl.BlockSpec(memory_space=pl.ANY)
    hx, hy, hz = max(nx - 1, 1), max(ny - 1, 1), max(nz - 1, 1)
    return pl.pallas_call(
        functools.partial(kernel, cfg),
        out_shape=jax.ShapeDtypeStruct((own, 256), F32),
        in_specs=[vspec] * 3 + [hspec] * 5,
        out_specs=vspec,
        scratch_shapes=[
            vmem((8, 128), F32),
            vmem((ne, 8, 128), F32),
            vmem(part, BF16),
            vmem((ne,) + part, BF16),
            vmem((512, width), BF16),
            vmem((512, width), BF16),
            vmem((128, width), BF16),
            vmem(tokens.shape, BF16),
            vmem((ne, main, width), BF16),
            vmem((ne, 16, width // tail_parts), BF16),
            vmem((n_rows, width), BF16),
            vmem((ne, 16, width // tail_parts), BF16),
            vmem((n_rows, 512), F32),
            vmem((ny, nx, nc, ne * r2, 128), F32),
            vmem((ne, 128, 128), BF16),
            vmem((ne, n_rows, 128), BF16),
            vmem((nx * n_rows, width // nx), BF16),
            vmem((nx, n_rows, 128), BF16),
            vmem((nx * n_rows, 256), BF16),
            vmem((ny, nz, nc, own, 256), F32),
            vmem((ny, nz, own, 256), BF16),
            vmem((ny, nz, own, 256), BF16),
            vmem((nz, own, 256), F32),
            vmem((hz, own, 256), BF16),
            vmem((hz, own, 256), BF16),
            vmem((hy, nz, own, 256), BF16),
            vmem((hy, nz, own, 256), BF16),
            dma((5,)),
            dma((2, ne - 1)),
            dma((2, ne - 1)),
            dma((2, nx, ne - 1)),
            dma((2, ne - 1)),
            dma((2, hx)),
            dma((2, ne - 1)),
            dma((2, hx)),
            dma((2, ny)),
            dma((2, 24)),
            dma((2, hy)),
            dma((2, hz)),
        ],
        compiler_params=pltpu.CompilerParams(
            collective_id=0, has_side_effects=True, vmem_limit_bytes=58 * 2**20
        ),
    )(ids, probs, tokens, *mats)


def body(cfg, tokens, expert_ids, gate_probs, w_gate, w_up, w_down, v_gate, v_up):
    ny, nz, nx, nc, ne, cap = cfg
    width = tokens.shape[1]
    total_tokens = tokens.shape[0] * ny * nz * nx * nc * ne
    mats = [w.reshape(128, width) for w in (w_gate, w_up, v_gate, v_up, w_down)]
    return fused(cfg, expert_ids.T, gate_probs.T, tokens, mats) * (1.0 / total_tokens)


def solution(mesh, grid=GRID):
    cfg = grid + (mesh.shape["expert"], 18)
    return jax.shard_map(
        functools.partial(body, cfg),
        mesh=mesh,
        in_specs=(
            P(("dp", "expert"), None),
            P(("dp", "expert"), None),
            P(("dp", "expert"), None),
            P("expert", None, None),
            P("expert", None, None),
            P("expert", None, None),
            P("expert", None, None),
            P("expert", None, None),
        ),
        out_specs=P("dp", "expert"),
        check_vma=False,
    )
```

```python
import functools

import jax
import jax.numpy as jnp
from jax import lax
from jax.experimental import pallas as pl
from jax.experimental.pallas import tpu as pltpu
from jax.sharding import PartitionSpec as P

F32 = jnp.float32
BF16 = jnp.bfloat16
GRID = (8, 3, 4, 2)


def iota(shape, dim):
    return lax.broadcasted_iota(jnp.int32, shape, dim)


def dot(a, b, dims=((1,), (0,)), precision=None):
    return lax.dot_general(a, b, (dims, ((), ())), precision=precision, preferred_element_type=F32)


def one_hot(mask):
    return jnp.where(mask, 1.0, 0.0).astype(BF16)


def kernel(
    cfg,
    ids_ref, probs_ref, tokens_ref, wg_ref, wu_ref, vg_ref, vu_ref, wd_ref,
    out_ref,
    meta_own, meta_all, part_own, parts, raw, weights, down, ordered, sent, sent_tail, rows, tails, pre,
    g_all, g_own, links, scaled_all, gathered, coef_all, coefs, partial, core_send, core_recv,
    z_acc, z_send, z_recv, ring_s, ring_r,
    w_sem, meta_sem, part_sem, row_sem, tail_sem, x_sem, sc_sem, coef_sem, core_sem, g_sem, rs_sem, z_sem,
):
    ny, nz, nx, nc, ne, cap = cfg
    width = tokens_ref.shape[1]
    slots = 2 * cap
    main = slots // 16 * 16
    rest = slots - main
    tail_parts = 16 // rest
    tw = width // tail_parts
    cw = width // nx
    n_rows = ne * slots
    n_main = ne * main
    n_tail = ne * 16
    plane = ny * nx * nc
    r2 = 128 // plane
    g_parts = 16 // r2
    pw = width // g_parts
    own = width // (ny * nz * nx * nc)

    dp = lax.axis_index("dp")
    e = lax.axis_index("expert")
    c = lax.rem(dp, nc)
    x = lax.rem(dp // nc, nx)
    zh = lax.rem(dp // (nc * nx), nz)
    y = dp // (nc * nx * nz)

    def at(yy=y, zz=zh, xx=x, cc=c):
        return ((yy * nz + zz) * nx + xx) * nc + cc

    def turn(v, k, n):
        return lax.rem(v + k + n, n)

    def remote(src, dst, s_sem, r_sem, dev):
        copy = pltpu.make_async_remote_copy(
            src_ref=src, dst_ref=dst, send_sem=s_sem, recv_sem=r_sem,
            device_id=dev, device_id_type=pl.DeviceIdType.MESH,
        )
        copy.start()
        return copy

    w_copies = []
    for m, ref in enumerate((wg_ref, wu_ref, vg_ref, vu_ref)):
        cp = pltpu.make_async_copy(ref, raw.at[pl.ds(m * 128, 128)], w_sem.at[m])
        cp.start()
        w_copies.append(cp)
    down_copy = pltpu.make_async_copy(wd_ref, down, w_sem.at[4])
    down_copy.start()

    peers = [(dp, turn(e, k, ne)) for k in range(1, ne)]
    for k in range(1, ny):
        peers.append((at(yy=turn(y, k, ny)), e))
    for k in range(1, nx):
        peers.append((at(xx=turn(x, k, nx)), e))
    for k in range(1, nz):
        peers.append((at(zz=turn(zh, k, nz)), e))
    for k in range(1, nc):
        peers.append((at(cc=turn(c, k, nc)), e))
    barrier = pltpu.get_barrier_semaphore()
    for dev in peers:
        pl.semaphore_signal(barrier, inc=1, device_id=dev, device_id_type=pl.DeviceIdType.MESH)

    lanes = 128
    upper = one_hot(iota((lanes, lanes), 0) < iota((lanes, lanes), 1))

    def slot_of(meta):
        ids = meta[0:1, :].astype(jnp.int32)
        hot = iota((2 * ne, lanes), 0) == ids
        before = dot(one_hot(hot), upper)
        where = before + cap * iota((2 * ne, lanes), 0).astype(F32)
        return jnp.sum(jnp.where(hot, where, 0.0), axis=0, keepdims=True).astype(jnp.int32)

    ids = ids_ref[...].astype(F32)
    probs = probs_ref[...]
    meta = jnp.concatenate(
        [
            jnp.concatenate([ids[0:1, :], ids[1:2, :]], axis=1),
            jnp.concatenate([probs[0:1, :], probs[1:2, :]], axis=1),
            jnp.zeros((6, lanes), F32),
        ],
        axis=0,
    )
    meta_own[...] = meta
    meta_all[e] = meta
    g_mine = slot_of(meta)
    half = one_hot(iota((lanes, lanes // 2), 0) % 64 == iota((lanes, lanes // 2), 1))
    r_main = iota((n_main, lanes), 0)
    slot_main = (r_main // main) * slots + r_main % main
    pick_main = dot(one_hot(slot_main == g_mine), half).astype(BF16)
    r_tail = iota((n_tail, lanes), 0)
    slot_tail = (r_tail // 16) * slots + main + r_tail % rest
    q_tail = (r_tail % 16) // rest
    hit_tail = slot_tail == g_mine

    def reorder(src, dst, rows_of):
        low = iota((rows_of, 128), 1) < 64

        def pair(m, carry):
            for h in range(nx // 2):
                first = src[:, pl.ds(pl.multiple_of((2 * m * (nx // 2) + h) * 128, 128), 128)]
                second = src[:, pl.ds(pl.multiple_of(((2 * m + 1) * (nx // 2) + h) * 128, 128), 128)]
                dst[:, pl.ds(pl.multiple_of(2 * h * cw + m * 128, 128), 128)] = jnp.where(
                    low, first, pltpu.roll(second, 64, 1)
                )
                dst[:, pl.ds(pl.multiple_of((2 * h + 1) * cw + m * 128, 128), 128)] = jnp.where(
                    low, pltpu.roll(first, 64, 1), second
                )
            return carry

        lax.fori_loop(0, ny * nz // 2, pair, 0)

    reorder(tokens_ref, ordered, tokens_ref.shape[0])

    order = [2, 1, 3, 0] if nx == 4 else list(range(1, nx)) + [0]
    z_order = (2, 1, 3) if ne == 4 else tuple(range(1, ne))

    def columns(k):
        return pl.ds(pl.multiple_of(turn(x, k, nx) * cw, 128), cw)

    def place_rows(k):
        val = dot(pick_main, ordered[:, columns(k)]).astype(BF16)
        for d in range(ne):
            sent[d, :, columns(k)] = val[d * main : (d + 1) * main]

    my_rows = pl.ds(pl.multiple_of(e * main, 16), main)

    def send_rows(k):
        got = []
        for j in z_order:
            d = turn(e, j, ne)
            got.append(
                remote(
                    sent.at[d, :, columns(k)], rows.at[my_rows, columns(k)],
                    row_sem.at[0, k, j - 1], row_sem.at[1, k, j - 1], (dp, d),
                )
            )
        rows[my_rows, columns(k)] = sent[e, :, columns(k)]
        return got

    place_rows(order[0])
    pl.semaphore_wait(barrier, len(peers))

    meta_copies, tail_copies, part_copies, row_copies = [], [], [], {}
    for j in range(1, ne):
        meta_copies.append(
            remote(meta_own, meta_all.at[e], meta_sem.at[0, j - 1], meta_sem.at[1, j - 1], (dp, turn(e, j, ne)))
        )
    row_copies[order[0]] = send_rows(order[0])
    down_copy.wait()
    s_row = iota((16, 128), 0)
    s_col = iota((16, 128), 1)
    first = ((y * nx + x) * nc + c) * r2
    for i in range(g_parts):
        pick = one_hot((s_row // r2 == i) & (s_col == first + s_row % r2))
        val = dot(pick, down[:, i * pw : (i + 1) * pw])
        part_val = val if i == 0 else part_val + val
    part_own[...] = part_val.astype(BF16)
    parts[e] = part_own[...]
    for j in z_order:
        part_copies.append(
            remote(part_own, parts.at[e], part_sem.at[0, j - 1], part_sem.at[1, j - 1], (dp, turn(e, j, ne)))
        )
    tail_val = jnp.zeros((n_tail, tw), F32)
    for q in range(tail_parts):
        pick = dot(one_hot(hit_tail & (q_tail == q)), half).astype(BF16)
        tail_val = tail_val + dot(pick, ordered[:, q * tw : (q + 1) * tw])
    tail_val = tail_val.astype(BF16)
    for d in range(ne):
        sent_tail[d] = tail_val[d * 16 : (d + 1) * 16]
    for j in z_order:
        d = turn(e, j, ne)
        tail_copies.append(
            remote(sent_tail.at[d], tails.at[e], tail_sem.at[0, j - 1], tail_sem.at[1, j - 1], (dp, d))
        )
    tails[e] = sent_tail[e]
    for k in order[1:]:
        place_rows(k)
        row_copies[k] = send_rows(k)

    for cp in tail_copies:
        cp.wait()
    t_row = iota((ne * rest, n_tail), 0)
    t_col = iota((ne * rest, n_tail), 1)
    flat_tails = tails[...].reshape(n_tail, tw)
    for q in range(tail_parts):
        hit = (t_row // rest == t_col // 16) & (t_col % 16 == q * rest + t_row % rest)
        rows[n_main:n_rows, q * tw : (q + 1) * tw] = dot(one_hot(hit), flat_tails).astype(BF16)

    def share(block, n, dev, base):
        return [
            remote(block, block, g_sem.at[0, base + k], g_sem.at[1, base + k], dev(k)) for k in range(1, n)
        ]

    def finish(copies):
        for cp in copies:
            cp.wait()

    x_rows = pl.ds(pl.multiple_of(x * n_rows, 16), n_rows)
    x_copies = []

    def forward(n):
        k = order[n]
        finish(row_copies[k])
        if k:
            x_copies.append(
                remote(
                    rows.at[:, columns(k)], gathered.at[x_rows], x_sem.at[0, k - 1], x_sem.at[1, k - 1],
                    (at(xx=turn(x, k, nx)), e),
                )
            )

    def multiply(n):
        k = order[n]
        val = dot(rows[:, columns(k)], weights[:, columns(k)], ((1,), (1,)))
        if n == 0:
            pre[...] = val
        else:
            pre[...] += val

    forward(0)

    for cp in part_copies:
        cp.wait()
    gw = parts[...].reshape(ne * 16, pw)
    acc = jnp.zeros((ne * 16, 128), F32)
    r_part = iota((ne * 16, 128), 0) % 16 // r2
    for i in range(g_parts):
        acc = acc + jnp.where(r_part == i, dot(gw, down[:, i * pw : (i + 1) * pw], ((1,), (1,))), 0.0)
    g_rows = ne * r2
    to_row = iota((g_rows, ne * 16), 0)
    from_row = iota((g_rows, ne * 16), 1)
    collect = jnp.where((from_row // 16 == to_row // r2) & (from_row % r2 == to_row % r2), 1.0, 0.0)
    g_all[y, x, c] = dot(collect, acc, precision=lax.Precision.HIGHEST)

    g_copies = share(g_all.at[y, x, c], nc, lambda k: (at(cc=turn(c, k, nc)), e), 0)
    finish(w_copies)
    reorder(raw, weights, 512)
    multiply(0)
    finish(g_copies)
    g_copies = share(g_all.at[y, x], nx, lambda k: (at(xx=turn(x, k, nx)), e), 8)
    for n in range(1, nx - 2):
        forward(n)
    finish(g_copies)
    g_copies = share(g_all.at[y], ny, lambda k: (at(yy=turn(y, k, ny)), e), 16)

    for n in range(1, nx - 2):
        multiply(n)

    finish(meta_copies)
    r_all = iota((n_rows, lanes), 0)
    in_main = r_all < n_main
    src_all = jnp.where(in_main, r_all // main, (r_all - n_main) // rest)
    slot_all = jnp.where(in_main, r_all % main, main + (r_all - n_main) % rest)
    same = one_hot(iota((lanes, lanes), 0) % 64 == iota((lanes, lanes), 1) % 64)
    g_src = [slot_of(meta_all[s]) for s in range(ne)]
    prob = jnp.zeros((n_rows, 1), F32)
    mine = []
    for s in range(ne):
        hit = (src_all == s) & (slot_all + e * slots == g_src[s])
        prob = prob + jnp.sum(jnp.where(hit, meta_all[s][1:2, :], 0.0), axis=1, keepdims=True)
        mine.append(dot(one_hot(hit), same).astype(BF16))
    for q in range(ne):
        total = jnp.zeros((n_rows, n_rows), F32)
        for s in range(ne):
            hit = one_hot((src_all == s) & (slot_all + q * slots == g_src[s]))
            total = total + dot(mine[s], hit, ((1,), (1,)))
        links[q] = total.astype(BF16)

    if nx > 2:
        forward(nx - 2)
        multiply(nx - 2)
    forward(nx - 1)
    multiply(nx - 1)

    gate_pre, up_pre = pre[:, 0:128], pre[:, 128:256]
    gate_tan, up_tan = pre[:, 256:384], pre[:, 384:512]
    sigmoid = jax.nn.sigmoid(gate_pre)
    silu_val = gate_pre * sigmoid
    slope_up = sigmoid * (1.0 + gate_pre * (1.0 - sigmoid)) * up_pre
    hidden_tan = slope_up * gate_tan + silu_val * up_tan
    valid = (iota((n_rows, 128), 1) // 64) == jnp.where(slot_all >= cap, 1, 0)
    low = iota((n_rows, 128), 1) < 64
    fold = n_rows // 2 + (-n_rows // 2) % 16
    scaled = jnp.where(valid, prob * hidden_tan, 0.0)
    both_halves = scaled + pltpu.roll(scaled, 64, 1)
    upper_rows = jnp.concatenate([both_halves[fold:], jnp.zeros((2 * fold - n_rows, 128), F32)], axis=0)
    scaled_all[e] = jnp.where(low[:fold], both_halves[:fold], upper_rows).astype(BF16)
    sc_copies = [
        remote(scaled_all.at[e], scaled_all.at[e], sc_sem.at[0, k - 1], sc_sem.at[1, k - 1], (dp, turn(e, k, ne)))
        for k in range(1, ne)
    ]
    finish(g_copies)
    flat_g = g_all[...].reshape(plane * g_rows, 128).astype(BF16)
    p_row = iota((128, plane * g_rows), 0)
    p_col = iota((128, plane * g_rows), 1)
    for q in range(ne):
        perm = one_hot(p_col == (p_row // r2) * g_rows + q * r2 + p_row % r2)
        g_own[q] = dot(perm, flat_g).astype(BF16)
    pulled = dot(dot(links[e], scaled.astype(BF16)).astype(BF16), g_own[e])
    gathered[x_rows] = rows[:, columns(0)]
    for k in range(1, ne):
        sc_copies[k - 1].wait()
        q = turn(e, -k, ne)
        packed = scaled_all[q].astype(F32)
        turned = pltpu.roll(packed, 64, 1)
        spread = jnp.concatenate(
            [jnp.where(low[:fold], packed, turned), jnp.where(low[:fold], turned, packed)[: n_rows - fold]], axis=0
        )
        spread = jnp.where(valid, spread, 0.0).astype(BF16)
        pulled = pulled + dot(dot(links[q], spread).astype(BF16), g_own[q])
    weighted = jnp.where(valid, prob * pulled, 0.0)
    coef_gate = weighted * slope_up
    coef_up = weighted * silu_val
    first_expert = slot_all < cap
    coef_mine = jnp.where(
        low,
        jnp.where(first_expert, coef_gate, pltpu.roll(coef_gate, 64, 1)),
        jnp.where(first_expert, pltpu.roll(coef_up, 64, 1), coef_up),
    ).astype(BF16)
    coef_all[x] = coef_mine
    coef_copies = [
        remote(coef_all.at[x], coef_all.at[x], coef_sem.at[0, k - 1], coef_sem.at[1, k - 1], (at(xx=turn(x, k, nx)), e))
        for k in range(1, nx)
    ]

    def place_coefs(i, val):
        here = pl.ds(pl.multiple_of(i * n_rows, 16), n_rows)
        coefs[here, 0:128] = jnp.where(first_expert, val, jnp.zeros_like(val))
        coefs[here, 128:256] = jnp.where(first_expert, jnp.zeros_like(val), val)

    place_coefs(x, coef_mine)
    finish(x_copies)
    for k in range(1, nx):
        coef_copies[k - 1].wait()
        i = turn(x, -k, nx)
        place_coefs(i, coef_all[i])

    span = cw // ny
    half_y = y // 2
    parity = y % 2
    pairs = [2, 1, 3, 0] if ny == 8 else list(range(1, ny // 2)) + [0]
    core_copies, y_copies = {}, {}

    def product(m):
        i = lax.rem(half_y + m, ny // 2)
        lhs = gathered[:, pl.ds(pl.multiple_of(i * 2 * span, 128), 2 * span)]
        part = dot(lhs, coefs[...], ((0,), (0,)))
        both = pl.ds(2 * i, 2)
        partial[both] = part.reshape(2, nz, nc, own, 256)
        if nc == 2:
            core_send[both] = partial[both, :, 1 - c].astype(BF16)
            core_copies[m] = remote(
                core_send.at[both], core_recv.at[both], core_sem.at[0, m], core_sem.at[1, m], (at(cc=1 - c), e)
            )

    def summed(t):
        val = partial[t, :, c]
        return val + core_recv[t].astype(F32) if nc == 2 else val

    def send_on(m):
        i = lax.rem(half_y + m, ny // 2)
        if nc == 2:
            core_copies[m].wait()
        for b in (1, 0):
            t = 2 * i + (parity + b) % 2
            j = 2 * m + b
            if j == 0:
                z_acc[...] = summed(t)
            else:
                ring_s[j - 1] = summed(t).astype(BF16)
                y_copies[j] = remote(
                    ring_s.at[j - 1], ring_r.at[j - 1], rs_sem.at[0, j - 1], rs_sem.at[1, j - 1], (at(yy=t), e)
                )

    for n, m in enumerate(pairs):
        product(m)
        if n:
            send_on(pairs[n - 1])
    send_on(pairs[-1])
    total = z_acc[...]
    for j, cp in y_copies.items():
        cp.wait()
        total = total + ring_r[j - 1].astype(F32)
    z_acc[...] = total

    result = z_acc[zh]
    z_copies = []
    for k in range(1, nz):
        t = turn(zh, k, nz)
        z_send[k - 1] = z_acc[t].astype(BF16)
        z_copies.append(
            remote(z_send.at[k - 1], z_recv.at[k - 1], z_sem.at[0, k - 1], z_sem.at[1, k - 1], (at(zz=t), e))
        )
    for k, cp in enumerate(z_copies):
        cp.wait()
        result = result + z_recv[k].astype(F32)
    out_ref[...] = result


def fused(cfg, ids, probs, tokens, mats):
    ny, nz, nx, nc, ne, cap = cfg
    width = tokens.shape[1]
    slots = 2 * cap
    main = slots // 16 * 16
    tail_parts = 16 // (slots - main)
    n_rows = ne * slots
    r2 = 128 // (ny * nx * nc)
    own = width // (ny * nz * nx * nc)
    part = (16, width * r2 // 16)
    vmem, dma = pltpu.VMEM, pltpu.SemaphoreType.DMA
    vspec = pl.BlockSpec(memory_space=pltpu.VMEM)
    hspec = pl.BlockSpec(memory_space=pl.ANY)
    hx, hy, hz = max(nx - 1, 1), max(ny - 1, 1), max(nz - 1, 1)
    return pl.pallas_call(
        functools.partial(kernel, cfg),
        out_shape=jax.ShapeDtypeStruct((own, 256), F32),
        in_specs=[vspec] * 3 + [hspec] * 5,
        out_specs=vspec,
        scratch_shapes=[
            vmem((8, 128), F32),
            vmem((ne, 8, 128), F32),
            vmem(part, BF16),
            vmem((ne,) + part, BF16),
            vmem((512, width), BF16),
            vmem((512, width), BF16),
            vmem((128, width), BF16),
            vmem(tokens.shape, BF16),
            vmem((ne, main, width), BF16),
            vmem((ne, 16, width // tail_parts), BF16),
            vmem((n_rows, width), BF16),
            vmem((ne, 16, width // tail_parts), BF16),
            vmem((n_rows, 512), F32),
            vmem((ny, nx, nc, ne * r2, 128), F32),
            vmem((ne, 128, 128), BF16),
            vmem((ne, n_rows, n_rows), BF16),
            vmem((ne, (n_rows // 2 + 15) // 16 * 16, 128), BF16),
            vmem((nx * n_rows, width // nx), BF16),
            vmem((nx, n_rows, 128), BF16),
            vmem((nx * n_rows, 256), BF16),
            vmem((ny, nz, nc, own, 256), F32),
            vmem((ny, nz, own, 256), BF16),
            vmem((ny, nz, own, 256), BF16),
            vmem((nz, own, 256), F32),
            vmem((hz, own, 256), BF16),
            vmem((hz, own, 256), BF16),
            vmem((hy, nz, own, 256), BF16),
            vmem((hy, nz, own, 256), BF16),
            dma((5,)),
            dma((2, ne - 1)),
            dma((2, ne - 1)),
            dma((2, nx, ne - 1)),
            dma((2, ne - 1)),
            dma((2, hx)),
            dma((2, ne - 1)),
            dma((2, hx)),
            dma((2, ny)),
            dma((2, 24)),
            dma((2, hy)),
            dma((2, hz)),
        ],
        compiler_params=pltpu.CompilerParams(
            collective_id=0, has_side_effects=True, vmem_limit_bytes=58 * 2**20
        ),
    )(ids, probs, tokens, *mats)


def body(cfg, tokens, expert_ids, gate_probs, w_gate, w_up, w_down, v_gate, v_up):
    ny, nz, nx, nc, ne, cap = cfg
    width = tokens.shape[1]
    total_tokens = tokens.shape[0] * ny * nz * nx * nc * ne
    mats = [w.reshape(128, width) for w in (w_gate, w_up, v_gate, v_up, w_down)]
    return fused(cfg, expert_ids.T, gate_probs.T, tokens, mats) * (1.0 / total_tokens)


def solution(mesh, grid=GRID):
    cfg = grid + (mesh.shape["expert"], 18)
    return jax.shard_map(
        functools.partial(body, cfg),
        mesh=mesh,
        in_specs=(
            P(("dp", "expert"), None),
            P(("dp", "expert"), None),
            P(("dp", "expert"), None),
            P("expert", None, None),
            P("expert", None, None),
            P("expert", None, None),
            P("expert", None, None),
            P("expert", None, None),
        ),
        out_specs=P("dp", "expert"),
        check_vma=False,
    )
```

```python
import functools

import jax
import jax.numpy as jnp
from jax import lax
from jax.experimental import pallas as pl
from jax.experimental.pallas import tpu as pltpu
from jax.sharding import PartitionSpec as P

F32 = jnp.float32
BF16 = jnp.bfloat16
GRID = (8, 3, 4, 2)


def iota(shape, dim):
    return lax.broadcasted_iota(jnp.int32, shape, dim)


def dot(a, b, dims=((1,), (0,)), precision=None):
    return lax.dot_general(a, b, (dims, ((), ())), precision=precision, preferred_element_type=F32)


def one_hot(mask):
    return jnp.where(mask, 1.0, 0.0).astype(BF16)


def kernel(
    cfg,
    ids_ref, probs_ref, tokens_hbm, wg_ref, wu_ref, vg_ref, vu_ref, wd_ref,
    out_ref,
    tokens_ref, meta_own, meta_all, part_own, parts, raw, weights, down, ordered, sent, sent_tail, rows, tails, pre,
    g_all, g_own, links, scaled_all, gathered, coef_all, coefs, partial, core_send, core_recv,
    z_acc, z_send, z_recv, ring_s, ring_r,
    w_sem, meta_sem, part_sem, row_sem, tail_sem, x_sem, sc_sem, coef_sem, core_sem, g_sem, rs_sem, z_sem,
):
    ny, nz, nx, nc, ne, cap = cfg
    width = tokens_ref.shape[1]
    slots = 2 * cap
    main = slots // 16 * 16
    rest = slots - main
    tail_parts = 16 // rest
    tw = width // tail_parts
    cw = width // nx
    n_rows = ne * slots
    n_main = ne * main
    n_tail = ne * 16
    plane = ny * nx * nc
    r2 = 128 // plane
    g_parts = 16 // r2
    pw = width // g_parts
    own = width // (ny * nz * nx * nc)

    dp = lax.axis_index("dp")
    e = lax.axis_index("expert")
    c = lax.rem(dp, nc)
    x = lax.rem(dp // nc, nx)
    zh = lax.rem(dp // (nc * nx), nz)
    y = dp // (nc * nx * nz)

    def at(yy=y, zz=zh, xx=x, cc=c):
        return ((yy * nz + zz) * nx + xx) * nc + cc

    def turn(v, k, n):
        return lax.rem(v + k + n, n)

    def remote(src, dst, s_sem, r_sem, dev):
        copy = pltpu.make_async_remote_copy(
            src_ref=src, dst_ref=dst, send_sem=s_sem, recv_sem=r_sem,
            device_id=dev, device_id_type=pl.DeviceIdType.MESH,
        )
        copy.start()
        return copy

    pending = []

    def arrived(copies):
        for cp in copies:
            cp.wait_recv()
            pending.append(cp)

    token_copy = pltpu.make_async_copy(tokens_hbm, tokens_ref, w_sem.at[5])
    token_copy.start()
    peers = [(dp, turn(e, k, ne)) for k in range(1, ne)]
    for k in range(1, ny):
        peers.append((at(yy=turn(y, k, ny)), e))
    for k in range(1, nx):
        peers.append((at(xx=turn(x, k, nx)), e))
    for k in range(1, nz):
        peers.append((at(zz=turn(zh, k, nz)), e))
    for k in range(1, nc):
        peers.append((at(cc=turn(c, k, nc)), e))
    barrier = pltpu.get_barrier_semaphore()
    for dev in peers:
        pl.semaphore_signal(barrier, inc=1, device_id=dev, device_id_type=pl.DeviceIdType.MESH)
    w_copies = []
    for m, ref in enumerate((wg_ref, wu_ref, vg_ref, vu_ref)):
        cp = pltpu.make_async_copy(ref, raw.at[pl.ds(m * 128, 128)], w_sem.at[m])
        cp.start()
        w_copies.append(cp)
    down_copy = pltpu.make_async_copy(wd_ref, down, w_sem.at[4])
    down_copy.start()


    lanes = 128
    upper = one_hot(iota((lanes, lanes), 0) < iota((lanes, lanes), 1))

    def slot_of(meta):
        ids = meta[0:1, :].astype(jnp.int32)
        hot = iota((2 * ne, lanes), 0) == ids
        before = dot(one_hot(hot), upper)
        where = before + cap * iota((2 * ne, lanes), 0).astype(F32)
        return jnp.sum(jnp.where(hot, where, 0.0), axis=0, keepdims=True).astype(jnp.int32)

    ids = ids_ref[...].astype(F32)
    probs = probs_ref[...]
    meta = jnp.concatenate(
        [
            jnp.concatenate([ids[0:1, :], ids[1:2, :]], axis=1),
            jnp.concatenate([probs[0:1, :], probs[1:2, :]], axis=1),
            jnp.zeros((6, lanes), F32),
        ],
        axis=0,
    )
    meta_own[...] = meta
    meta_all[e] = meta
    g_mine = slot_of(meta)
    half = one_hot(iota((lanes, lanes // 2), 0) % 64 == iota((lanes, lanes // 2), 1))
    r_main = iota((n_main, lanes), 0)
    slot_main = (r_main // main) * slots + r_main % main
    pick_main = dot(one_hot(slot_main == g_mine), half).astype(BF16)
    r_tail = iota((n_tail, lanes), 0)
    slot_tail = (r_tail // 16) * slots + main + r_tail % rest
    q_tail = (r_tail % 16) // rest
    hit_tail = slot_tail == g_mine

    def reorder(src, dst, rows_of):
        low = iota((rows_of, 128), 1) < 64

        def pair(m, carry):
            for h in range(nx // 2):
                first = src[:, pl.ds(pl.multiple_of((2 * m * (nx // 2) + h) * 128, 128), 128)]
                second = src[:, pl.ds(pl.multiple_of(((2 * m + 1) * (nx // 2) + h) * 128, 128), 128)]
                dst[:, pl.ds(pl.multiple_of(2 * h * cw + m * 128, 128), 128)] = jnp.where(
                    low, first, pltpu.roll(second, 64, 1)
                )
                dst[:, pl.ds(pl.multiple_of((2 * h + 1) * cw + m * 128, 128), 128)] = jnp.where(
                    low, pltpu.roll(first, 64, 1), second
                )
            return carry

        lax.fori_loop(0, ny * nz // 2, pair, 0)

    token_copy.wait()
    reorder(tokens_ref, ordered, tokens_ref.shape[0])

    order = [2, 1, 3, 0] if nx == 4 else list(range(1, nx)) + [0]
    z_order = (2, 1, 3) if ne == 4 else tuple(range(1, ne))

    def columns(k):
        return pl.ds(pl.multiple_of(turn(x, k, nx) * cw, 128), cw)

    def pieces(k):
        if k or cw % 256:
            return [(k, columns(k))]
        start = x * cw
        return [(s, pl.ds(pl.multiple_of(start + h * (cw // 2), 128), cw // 2)) for h, s in ((0, 0), (1, nx))]

    def place_rows(k):
        val = dot(pick_main, ordered[:, columns(k)]).astype(BF16)
        for d in range(ne):
            sent[d, :, columns(k)] = val[d * main : (d + 1) * main]

    my_rows = pl.ds(pl.multiple_of(e * main, 16), main)

    def send_rows(k):
        rows[my_rows, columns(k)] = sent[e, :, columns(k)]
        return [
            remote(
                sent.at[turn(e, j, ne), :, part], rows.at[my_rows, part],
                row_sem.at[0, s, j - 1], row_sem.at[1, s, j - 1], (dp, turn(e, j, ne)),
            )
            for s, part in pieces(k)
            for j in z_order
        ]

    place_rows(order[0])
    pl.semaphore_wait(barrier, len(peers))

    meta_copies, tail_copies, part_copies, row_copies = [], [], [], {}
    for j in range(1, ne):
        meta_copies.append(
            remote(meta_own, meta_all.at[e], meta_sem.at[0, j - 1], meta_sem.at[1, j - 1], (dp, turn(e, j, ne)))
        )
    row_copies[order[0]] = send_rows(order[0])
    down_copy.wait()
    s_row = iota((16, 128), 0)
    s_col = iota((16, 128), 1)
    first = ((y * nx + x) * nc + c) * r2
    for i in range(g_parts):
        pick = one_hot((s_row // r2 == i) & (s_col == first + s_row % r2))
        val = dot(pick, down[:, i * pw : (i + 1) * pw])
        part_val = val if i == 0 else part_val + val
    part_own[...] = part_val.astype(BF16)
    parts[e] = part_own[...]
    for j in z_order:
        part_copies.append(
            remote(part_own, parts.at[e], part_sem.at[0, j - 1], part_sem.at[1, j - 1], (dp, turn(e, j, ne)))
        )
    tail_val = jnp.zeros((n_tail, tw), F32)
    for q in range(tail_parts):
        pick = dot(one_hot(hit_tail & (q_tail == q)), half).astype(BF16)
        tail_val = tail_val + dot(pick, ordered[:, q * tw : (q + 1) * tw])
    tail_val = tail_val.astype(BF16)
    for d in range(ne):
        sent_tail[d] = tail_val[d * 16 : (d + 1) * 16]
    for j in z_order:
        d = turn(e, j, ne)
        tail_copies.append(
            remote(sent_tail.at[d], tails.at[e], tail_sem.at[0, j - 1], tail_sem.at[1, j - 1], (dp, d))
        )
    tails[e] = sent_tail[e]
    for k in order[1:]:
        place_rows(k)
        row_copies[k] = send_rows(k)

    arrived(tail_copies)
    t_row = iota((ne * rest, n_tail), 0)
    t_col = iota((ne * rest, n_tail), 1)
    flat_tails = tails[...].reshape(n_tail, tw)
    for q in range(tail_parts):
        hit = (t_row // rest == t_col // 16) & (t_col % 16 == q * rest + t_row % rest)
        rows[n_main:n_rows, q * tw : (q + 1) * tw] = dot(one_hot(hit), flat_tails).astype(BF16)

    def share(block, n, dev, base):
        return [
            remote(block, block, g_sem.at[0, base + k], g_sem.at[1, base + k], dev(k)) for k in range(1, n)
        ]

    x_rows = pl.ds(pl.multiple_of(x * n_rows, 16), n_rows)
    x_copies = []

    def forward(n):
        k = order[n]
        arrived(row_copies[k])
        if k:
            x_copies.append(
                remote(
                    rows.at[:, columns(k)], gathered.at[x_rows], x_sem.at[0, k - 1], x_sem.at[1, k - 1],
                    (at(xx=turn(x, k, nx)), e),
                )
            )

    def multiply(n):
        k = order[n]
        for _, part in pieces(k):
            val = dot(rows[:, part], weights[:, part], ((1,), (1,)))
            if n == 0:
                pre[...] = val
            else:
                pre[...] += val

    forward(0)

    arrived(part_copies)
    gw = parts[...].reshape(ne * 16, pw)
    acc = jnp.zeros((ne * 16, 128), F32)
    r_part = iota((ne * 16, 128), 0) % 16 // r2
    for i in range(g_parts):
        acc = acc + jnp.where(r_part == i, dot(gw, down[:, i * pw : (i + 1) * pw], ((1,), (1,))), 0.0)
    g_rows = ne * r2
    to_row = iota((g_rows, ne * 16), 0)
    from_row = iota((g_rows, ne * 16), 1)
    collect = jnp.where((from_row // 16 == to_row // r2) & (from_row % r2 == to_row % r2), 1.0, 0.0)
    g_all[y, x, c] = dot(collect, acc, precision=lax.Precision.HIGHEST)

    g_copies = share(g_all.at[y, x, c], nc, lambda k: (at(cc=turn(c, k, nc)), e), 0)
    for cp in w_copies:
        cp.wait()
    reorder(raw, weights, 512)
    multiply(0)
    arrived(g_copies)
    g_copies = share(g_all.at[y, x], nx, lambda k: (at(xx=turn(x, k, nx)), e), 8)
    for n in range(1, nx - 2):
        forward(n)
    arrived(g_copies)
    g_copies = share(g_all.at[y], ny, lambda k: (at(yy=turn(y, k, ny)), e), 16)

    for n in range(1, nx - 2):
        multiply(n)

    arrived(meta_copies)
    r_all = iota((n_rows, lanes), 0)
    in_main = r_all < n_main
    src_all = jnp.where(in_main, r_all // main, (r_all - n_main) // rest)
    slot_all = jnp.where(in_main, r_all % main, main + (r_all - n_main) % rest)
    same = one_hot(iota((lanes, lanes), 0) % 64 == iota((lanes, lanes), 1) % 64)
    g_src = [slot_of(meta_all[s]) for s in range(ne)]
    prob = jnp.zeros((n_rows, 1), F32)
    mine = []
    for s in range(ne):
        hit = (src_all == s) & (slot_all + e * slots == g_src[s])
        prob = prob + jnp.sum(jnp.where(hit, meta_all[s][1:2, :], 0.0), axis=1, keepdims=True)
        mine.append(dot(one_hot(hit), same).astype(BF16))
    for q in range(ne):
        total = jnp.zeros((n_rows, n_rows), F32)
        for s in range(ne):
            hit = one_hot((src_all == s) & (slot_all + q * slots == g_src[s]))
            total = total + dot(mine[s], hit, ((1,), (1,)))
        links[q] = total.astype(BF16)

    if nx > 2:
        forward(nx - 2)
        multiply(nx - 2)
    for h, (_, part) in enumerate(pieces(0)):
        arrived(row_copies[0][h * (ne - 1) : (h + 1) * (ne - 1)])
        pre[...] += dot(rows[:, part], weights[:, part], ((1,), (1,)))

    gate_pre, up_pre = pre[:, 0:128], pre[:, 128:256]
    gate_tan, up_tan = pre[:, 256:384], pre[:, 384:512]
    sigmoid = jax.nn.sigmoid(gate_pre)
    silu_val = gate_pre * sigmoid
    slope_up = sigmoid * (1.0 + gate_pre * (1.0 - sigmoid)) * up_pre
    hidden_tan = slope_up * gate_tan + silu_val * up_tan
    valid = (iota((n_rows, 128), 1) // 64) == jnp.where(slot_all >= cap, 1, 0)
    low = iota((n_rows, 128), 1) < 64
    fold = n_rows // 2 + (-n_rows // 2) % 16
    scaled = jnp.where(valid, prob * hidden_tan, 0.0)
    both_halves = scaled + pltpu.roll(scaled, 64, 1)
    upper_rows = jnp.concatenate([both_halves[fold:], jnp.zeros((2 * fold - n_rows, 128), F32)], axis=0)
    scaled_all[e] = jnp.where(low[:fold], both_halves[:fold], upper_rows).astype(BF16)
    sc_copies = [
        remote(scaled_all.at[e], scaled_all.at[e], sc_sem.at[0, k - 1], sc_sem.at[1, k - 1], (dp, turn(e, k, ne)))
        for k in range(1, ne)
    ]
    arrived(g_copies)
    flat_g = g_all[...].reshape(plane * g_rows, 128).astype(BF16)
    p_row = iota((128, plane * g_rows), 0)
    p_col = iota((128, plane * g_rows), 1)
    for q in range(ne):
        perm = one_hot(p_col == (p_row // r2) * g_rows + q * r2 + p_row % r2)
        g_own[q] = dot(perm, flat_g).astype(BF16)
    pulled = dot(dot(links[e], scaled.astype(BF16)).astype(BF16), g_own[e])
    gathered[x_rows] = rows[:, columns(0)]
    for k in range(1, ne):
        arrived(sc_copies[k - 1 : k])
        q = turn(e, -k, ne)
        packed = scaled_all[q].astype(F32)
        turned = pltpu.roll(packed, 64, 1)
        spread = jnp.concatenate(
            [jnp.where(low[:fold], packed, turned), jnp.where(low[:fold], turned, packed)[: n_rows - fold]], axis=0
        )
        spread = jnp.where(valid, spread, 0.0).astype(BF16)
        pulled = pulled + dot(dot(links[q], spread).astype(BF16), g_own[q])
    weighted = jnp.where(valid, prob * pulled, 0.0)
    coef_gate = weighted * slope_up
    coef_up = weighted * silu_val
    first_expert = slot_all < cap
    coef_mine = jnp.where(
        low,
        jnp.where(first_expert, coef_gate, pltpu.roll(coef_gate, 64, 1)),
        jnp.where(first_expert, pltpu.roll(coef_up, 64, 1), coef_up),
    ).astype(BF16)
    coef_all[x] = coef_mine
    coef_copies = [
        remote(coef_all.at[x], coef_all.at[x], coef_sem.at[0, k - 1], coef_sem.at[1, k - 1], (at(xx=turn(x, k, nx)), e))
        for k in range(1, nx)
    ]

    def place_coefs(i, val):
        here = pl.ds(pl.multiple_of(i * n_rows, 16), n_rows)
        coefs[here, 0:128] = jnp.where(first_expert, val, jnp.zeros_like(val))
        coefs[here, 128:256] = jnp.where(first_expert, jnp.zeros_like(val), val)

    place_coefs(x, coef_mine)
    arrived(x_copies)
    for k in range(1, nx):
        arrived(coef_copies[k - 1 : k])
        i = turn(x, -k, nx)
        place_coefs(i, coef_all[i])

    span = cw // ny
    half_y = y // 2
    parity = y % 2
    pairs = [2, 1, 3, 0] if ny == 8 else list(range(1, ny // 2)) + [0]
    core_copies, y_copies = {}, {}

    def product(m):
        i = lax.rem(half_y + m, ny // 2)
        lhs = gathered[:, pl.ds(pl.multiple_of(i * 2 * span, 128), 2 * span)]
        part = dot(lhs, coefs[...], ((0,), (0,)))
        both = pl.ds(2 * i, 2)
        partial[both] = part.reshape(2, nz, nc, own, 256)
        if nc == 2:
            core_send[both] = partial[both, :, 1 - c].astype(BF16)
            core_copies[m] = remote(
                core_send.at[both], core_recv.at[both], core_sem.at[0, m], core_sem.at[1, m], (at(cc=1 - c), e)
            )

    def summed(t):
        val = partial[t, :, c]
        return val + core_recv[t].astype(F32) if nc == 2 else val

    def send_on(m):
        i = lax.rem(half_y + m, ny // 2)
        if nc == 2:
            arrived([core_copies[m]])
        for b in (1, 0):
            t = 2 * i + (parity + b) % 2
            j = 2 * m + b
            if j == 0:
                z_acc[...] = summed(t)
            else:
                ring_s[j - 1] = summed(t).astype(BF16)
                y_copies[j] = remote(
                    ring_s.at[j - 1], ring_r.at[j - 1], rs_sem.at[0, j - 1], rs_sem.at[1, j - 1], (at(yy=t), e)
                )

    for n, m in enumerate(pairs):
        product(m)
        if n:
            send_on(pairs[n - 1])
    send_on(pairs[-1])
    total = z_acc[...]
    for j, cp in y_copies.items():
        arrived([cp])
        total = total + ring_r[j - 1].astype(F32)
    z_acc[...] = total

    result = z_acc[zh]
    z_copies = []
    for k in range(1, nz):
        t = turn(zh, k, nz)
        z_send[k - 1] = z_acc[t].astype(BF16)
        z_copies.append(
            remote(z_send.at[k - 1], z_recv.at[k - 1], z_sem.at[0, k - 1], z_sem.at[1, k - 1], (at(zz=t), e))
        )
    for k, cp in enumerate(z_copies):
        arrived([cp])
        result = result + z_recv[k].astype(F32)
    out_ref[...] = result
    for cp in pending:
        cp.wait_send()


def fused(cfg, ids, probs, tokens, mats):
    ny, nz, nx, nc, ne, cap = cfg
    width = tokens.shape[1]
    slots = 2 * cap
    main = slots // 16 * 16
    tail_parts = 16 // (slots - main)
    n_rows = ne * slots
    r2 = 128 // (ny * nx * nc)
    own = width // (ny * nz * nx * nc)
    part = (16, width * r2 // 16)
    vmem, dma = pltpu.VMEM, pltpu.SemaphoreType.DMA
    vspec = pl.BlockSpec(memory_space=pltpu.VMEM)
    hspec = pl.BlockSpec(memory_space=pl.ANY)
    hx, hy, hz = max(nx - 1, 1), max(ny - 1, 1), max(nz - 1, 1)
    return pl.pallas_call(
        functools.partial(kernel, cfg),
        out_shape=jax.ShapeDtypeStruct((own, 256), F32),
        in_specs=[vspec] * 2 + [hspec] * 6,
        out_specs=vspec,
        scratch_shapes=[
            vmem(tokens.shape, BF16),
            vmem((8, 128), F32),
            vmem((ne, 8, 128), F32),
            vmem(part, BF16),
            vmem((ne,) + part, BF16),
            vmem((512, width), BF16),
            vmem((512, width), BF16),
            vmem((128, width), BF16),
            vmem(tokens.shape, BF16),
            vmem((ne, main, width), BF16),
            vmem((ne, 16, width // tail_parts), BF16),
            vmem((n_rows, width), BF16),
            vmem((ne, 16, width // tail_parts), BF16),
            vmem((n_rows, 512), F32),
            vmem((ny, nx, nc, ne * r2, 128), F32),
            vmem((ne, 128, 128), BF16),
            vmem((ne, n_rows, n_rows), BF16),
            vmem((ne, (n_rows // 2 + 15) // 16 * 16, 128), BF16),
            vmem((nx * n_rows, width // nx), BF16),
            vmem((nx, n_rows, 128), BF16),
            vmem((nx * n_rows, 256), BF16),
            vmem((ny, nz, nc, own, 256), F32),
            vmem((ny, nz, own, 256), BF16),
            vmem((ny, nz, own, 256), BF16),
            vmem((nz, own, 256), F32),
            vmem((hz, own, 256), BF16),
            vmem((hz, own, 256), BF16),
            vmem((hy, nz, own, 256), BF16),
            vmem((hy, nz, own, 256), BF16),
            dma((6,)),
            dma((2, ne - 1)),
            dma((2, ne - 1)),
            dma((2, nx + 1, ne - 1)),
            dma((2, ne - 1)),
            dma((2, hx)),
            dma((2, ne - 1)),
            dma((2, hx)),
            dma((2, ny)),
            dma((2, 24)),
            dma((2, hy)),
            dma((2, hz)),
        ],
        compiler_params=pltpu.CompilerParams(
            collective_id=0, has_side_effects=True, vmem_limit_bytes=58 * 2**20
        ),
    )(ids, probs, tokens, *mats)


def body(cfg, tokens, expert_ids, gate_probs, w_gate, w_up, w_down, v_gate, v_up):
    ny, nz, nx, nc, ne, cap = cfg
    width = tokens.shape[1]
    total_tokens = tokens.shape[0] * ny * nz * nx * nc * ne
    mats = [w.reshape(128, width) for w in (w_gate, w_up, v_gate, v_up, w_down)]
    return fused(cfg, expert_ids.T, gate_probs.T, tokens, mats) * (1.0 / total_tokens)


def solution(mesh, grid=GRID):
    cfg = grid + (mesh.shape["expert"], 18)
    return jax.shard_map(
        functools.partial(body, cfg),
        mesh=mesh,
        in_specs=(
            P(("dp", "expert"), None),
            P(("dp", "expert"), None),
            P(("dp", "expert"), None),
            P("expert", None, None),
            P("expert", None, None),
            P("expert", None, None),
            P("expert", None, None),
            P("expert", None, None),
        ),
        out_specs=P("dp", "expert"),
        check_vma=False,
    )
```
